32 devices in a mesh: ctx: 8 (over y, x, core), head: 4 (over z).
Axes of the slice: x: 2, y: 2, z: 4, core: 2. Of those that a mesh axis runs over, the one named last changes fastest.
Arguments:
- tokens: bfloat16 [8192, 4096], P('ctx', 'head'), may hold values from -23 to 23
- proj_weight: bfloat16 [4096, 32, 384], P(None, 'head'), may hold values from -1 to 1
- partner_shard: int32 [32, 128, 3], P('head'), may hold values from 0 to 7, all different within a row; in each aligned block of 16 rows (0 to 15, 16 to 31, ..., all dimensions but the last counted through in order) at most 12 rows name the same one
- partner_block: int32 [32, 128, 3], P('head'), may hold values from 0 to 15
Outputs:
- attended: bfloat16 [8192, 32, 128], P('ctx', 'head')
The draws below stay inside these ranges and needn't reach their ends.
Inputs may be any that keep to these rules, and one draw needn't show every extreme that they name: `partner_shard`: the 3 entries of one row differ. For each head, within each aligned run of 16 block rows, no value is named more than 12 times, and some runs name one value exactly 12 times.
All inputs are finite; a program needn't handle non-finite values.
Results may differ from the reference program's by a relative error of at most 0.008.
Values may be sent and summed in bfloat16 or wider, within the bound.
No kernel may reach another device: no remote copies, remote signals or barrier semaphores. Data moves between devices by JAX's collectives and lax.ppermute only.
A program may use at most 192 MiB of HBM per device.

```python
import math
import jax
import jax.numpy as jnp
import numpy as np
from jax import lax

D = 4096
NH = 32
HEAD_DIMENSION = 128
BLK = 64
GLOB = 2
RAND = 3
BPD = 16
SEQUENCE_TOKENS = 8192
NB = 128
MOST = 12
N_CTX = 8


def draw_tokens(key, part):
    key_base = jax.random.fold_in(jax.random.fold_in(key, 11), 0)
    values = jax.random.truncated_normal(key_base, -4.0, 4.0, (SEQUENCE_TOKENS, D), jnp.float32)
    return values.astype(jnp.bfloat16)


def draw_proj_weight(key, part):
    values = jax.random.truncated_normal(jax.random.fold_in(key, 23), -4.0, 4.0, (D, NH, 3 * HEAD_DIMENSION), jnp.float32) * D ** (-0.5)
    return values.astype(jnp.bfloat16)


def plant(drawn, stream_key, least, high):
    place = [jax.random.randint(jax.random.fold_in(stream_key, axis), (), 0, length) for axis, length in enumerate(drawn.shape)]
    main_axis = drawn.shape.index(max(drawn.shape))
    beside = place[:main_axis] + [(place[main_axis] + 1) % drawn.shape[main_axis]] + place[main_axis + 1:]
    return drawn.at[tuple(place)].set(least).at[tuple(beside)].set(high)


def routed_block(rng, own, number, rows, number_of, top, most, lean):
    order = jax.random.permutation(rng, number_of)
    heavy_load, usual = portions_of(number_of, rows * top, most, lean, True), portions_of(number_of, rows * top, most, lean, False)
    places = jnp.arange(number_of)

    def named(tallies, rotation):
        used = int((tallies > 0).sum())
        fixed = max(1, used // 4)
        shifted = fixed + (places - fixed + rotation * (used - fixed)) % max(1, number_of - fixed)
        return jnp.zeros((number_of,), jnp.int32).at[order[jnp.where(places < fixed, places, shifted)]].set(jnp.asarray(tallies, jnp.int32))

    tallies = jnp.where(number % 4 == 0, named(heavy_load, number // 4), named(usual, number - number // 4 - 1))
    mixed = jax.random.permutation(jax.random.fold_in(own, 3), number_of)
    giver, taker = mixed[0:number_of // 2 * 2:2], mixed[1:number_of // 2 * 2:2]
    slack = jnp.minimum(tallies[giver] - 1, most - tallies[taker]) // 2
    slack = jnp.where((giver == order[0]) | (taker == order[0]) | (tallies[taker] == 0), 0, jnp.maximum(slack, 0))
    shifted = jax.random.randint(jax.random.fold_in(own, 4), (number_of // 2,), 0, 1 << 20) % (slack + 1)
    tallies = tallies.at[giver].add(-shifted).at[taker].add(shifted)
    items = jnp.searchsorted(jnp.cumsum(tallies), jnp.arange(rows * top), side="right").astype(jnp.int32)
    table = items.reshape(top, rows).T
    table = table[jax.random.permutation(jax.random.fold_in(own, 1), rows)]
    rotation = jax.random.randint(jax.random.fold_in(own, 2), (rows, 1), 0, top)
    return jnp.take_along_axis(table, (jnp.arange(top)[None, :] + rotation) % top, axis=1)


def portions_of(number_of, total, most, slope, full):
    portions = [(1 << 20) // math.isqrt(standing ** slope) + 1 for standing in range(1, number_of + 1)]
    largest = most if full else min(most, max(-(-total // number_of), total * portions[0] // sum(portions)))
    least = 1 if total - largest >= number_of - 1 else 0
    holding, rest = [largest] + [least] * (number_of - 1), total - largest - least * (number_of - 1)
    while rest > 0:
        candidates = [i for i in range(1, number_of) if holding[i] < largest] or [i for i in range(1, number_of) if holding[i] < most]
        mass, budget = sum([portions[i] for i in candidates]), rest
        for i in candidates:
            extra = min(most - holding[i], max(1, budget * portions[i] // mass), rest)
            holding[i] = holding[i] + extra
            rest = rest - extra
    return np.array(holding)


def setup_inputs(seed: int = 0) -> dict:
    arg_keys = jax.random.split(jax.random.key(seed), 5)
    tokens = draw_tokens(jax.random.fold_in(arg_keys[4], 71), 0)
    proj_weight = draw_proj_weight(jax.random.fold_in(arg_keys[4], 71), 0)
    partner_shard_keys = jax.random.split(jax.random.fold_in(arg_keys[2], 1), NH * NB // BPD)
    partner_shard_turns = jax.random.permutation(jax.random.fold_in(arg_keys[2], 3), NH * NB // BPD)
    partner_shard = jax.vmap(lambda own, number: routed_block(jax.random.fold_in(arg_keys[2], 2), own, number, BPD, N_CTX, RAND, MOST, 2))(partner_shard_keys, partner_shard_turns).reshape((NH, NB, RAND))
    partner_block = plant(jax.random.randint(arg_keys[3], (NH, NB, RAND), 0, BPD), jax.random.fold_in(arg_keys[3], 1), 0, BPD - 1).astype(jnp.int32)
    return {"tokens": tokens, "proj_weight": proj_weight, "partner_shard": partner_shard, "partner_block": partner_block}


def reference(tokens, proj_weight, partner_shard, partner_block):
    flat_weight = proj_weight.reshape(D, NH * 3 * HEAD_DIMENSION)
    packed = jnp.dot(tokens, flat_weight, preferred_element_type=jnp.float32).astype(jnp.bfloat16)
    packed = jnp.transpose(packed.reshape(SEQUENCE_TOKENS, NH, 3 * HEAD_DIMENSION), (1, 0, 2))
    partner = (partner_shard * BPD + partner_block).astype(jnp.int32)
    inverse_root_scale = HEAD_DIMENSION ** -0.5

    def one_head(inputs):
        head_pack, indices = inputs
        head_pack = head_pack.astype(jnp.float32)
        queries = head_pack[:, :HEAD_DIMENSION]
        keys = head_pack[:, HEAD_DIMENSION:2 * HEAD_DIMENSION]
        values = head_pack[:, 2 * HEAD_DIMENSION:]
        blocked_query_rows = queries.reshape(NB, BLK, HEAD_DIMENSION)

        def gather_set(field):
            field_blocks = field.reshape(NB, BLK, HEAD_DIMENSION)
            leading = jnp.broadcast_to(field_blocks[:GLOB].reshape(1, GLOB * BLK, HEAD_DIMENSION), (NB, GLOB * BLK, HEAD_DIMENSION))
            partners = field_blocks[indices].reshape(NB, RAND * BLK, HEAD_DIMENSION)
            return jnp.concatenate([jnp.roll(field_blocks, 1, 0), field_blocks, jnp.roll(field_blocks, -1, 0), leading, partners], axis=1)

        partner_key_rows = gather_set(keys)
        partner_value_rows = gather_set(values)
        logit_scores = jnp.einsum("msx,mix->msi", blocked_query_rows, partner_key_rows, precision=lax.Precision.HIGHEST) * inverse_root_scale
        softmax_weight_matrix = jax.nn.softmax(logit_scores, axis=-1).astype(jnp.bfloat16)
        softmax_weight_matrix = lax.optimization_barrier(softmax_weight_matrix).astype(jnp.float32)
        sparse_attention_output = jnp.einsum("thw,twp->thp", softmax_weight_matrix, partner_value_rows, precision=lax.Precision.HIGHEST).reshape(SEQUENCE_TOKENS, HEAD_DIMENSION)
        global_scores = jnp.dot(queries[:GLOB * BLK], keys.T, precision=lax.Precision.HIGHEST) * inverse_root_scale
        global_weights = jax.nn.softmax(global_scores, axis=-1)
        global_out = jnp.dot(global_weights, values, precision=lax.Precision.HIGHEST)
        context = jnp.concatenate([global_out, sparse_attention_output[GLOB * BLK:]], axis=0)
        return context.astype(jnp.bfloat16)

    result = lax.map(one_head, (packed, partner))
    return jnp.transpose(result, (1, 0, 2))
```

```python
import functools

import jax
import jax.numpy as jnp
from jax import lax
from jax.experimental import pallas as pl
from jax.experimental.pallas import tpu as pltpu
from jax.sharding import PartitionSpec as P

HEAD_DIMENSION = 128
BLK = 64
GLOB = 2
RAND = 3
KEY_SET = 3 + GLOB + RAND
LEAD = GLOB * BLK
EXPONENT = HEAD_DIMENSION ** (-0.5) * 1.4426950408889634
PARTS = (4, 4, 4, 4)
TOGETHER = 8
TRANSPOSED = (((1,), (1,)), ((), ()))


def project_kernel(x_ref, w_ref, *refs):
    q_ref, kv_ref = refs[-2:]
    out = jnp.dot(x_ref[...], w_ref[...], preferred_element_type=jnp.float32).astype(jnp.bfloat16)
    for i in range(out.shape[1] // (3 * HEAD_DIMENSION)):
        at = i * 3 * HEAD_DIMENSION
        q_ref[:, i * HEAD_DIMENSION : (i + 1) * HEAD_DIMENSION] = out[:, at : at + HEAD_DIMENSION]
        kv_ref[:, 2 * i * HEAD_DIMENSION : 2 * (i + 1) * HEAD_DIMENSION] = out[
            :, at + HEAD_DIMENSION : at + 3 * HEAD_DIMENSION
        ]


def project(x, weight, queries, start, total, after):
    rows, depth = x.shape
    heads = weight.shape[1] // (3 * HEAD_DIMENSION)
    per = 2
    at = start // rows
    assert at * rows == start
    given = () if queries is None else (queries,)
    return pl.pallas_call(
        project_kernel,
        grid=(heads // per,),
        in_specs=[
            pl.BlockSpec((rows, depth), lambda i: (0, 0)),
            pl.BlockSpec((depth, per * 3 * HEAD_DIMENSION), lambda i: (0, i)),
        ]
        + [pl.BlockSpec(memory_space=pltpu.HBM)] * (len(given) + len(after)),
        out_specs=[
            pl.BlockSpec((rows, per * HEAD_DIMENSION), lambda i: (at, i)),
            pl.BlockSpec((rows, per * 2 * HEAD_DIMENSION), lambda i: (0, i)),
        ],
        out_shape=[
            jax.ShapeDtypeStruct((total, heads * HEAD_DIMENSION), jnp.bfloat16),
            jax.ShapeDtypeStruct((rows, heads * 2 * HEAD_DIMENSION), jnp.bfloat16),
        ],
        input_output_aliases={2: 0} if given else {},
        compiler_params=pltpu.CompilerParams(vmem_limit_bytes=40 << 20),
    )(x, weight, *given, *after)


def column_copies(sources, places, head, target, sem):
    at = pl.multiple_of(head * 2 * HEAD_DIMENSION, 2 * HEAD_DIMENSION)
    return [
        pltpu.make_async_copy(
            ref.at[:, pl.ds(at, 2 * HEAD_DIMENSION)], target.at[pl.ds(place, ref.shape[0]), :], sem
        )
        for ref, place in zip(sources, places)
    ]


def sparse_kernel(places, heads, blocks, at_ref, q_ref, *refs):
    sources, (o_ref, held, sem) = refs[: len(places)], refs[len(places) :]
    head = pl.program_id(0)
    slot = lax.rem(head, 2)

    def copies(which, into):
        return column_copies(sources, places, which, held.at[into], sem.at[into])

    @pl.when(head == 0)
    def _():
        for copy in copies(head, slot):
            copy.start()

    @pl.when(head + 1 < heads)
    def _():
        for copy in copies(head + 1, 1 - slot):
            copy.start()

    for copy in copies(head, slot):
        copy.wait()

    def step(group, carry):
        rows, keys, scores, weights, totals = [], [], [], [], []
        for i in range(TOGETHER):
            block = group * TOGETHER + i
            rows.append(pl.ds(pl.multiple_of(block * BLK, BLK), BLK))
            keys.append(
                jnp.concatenate(
                    [
                        held[
                            slot,
                            pl.ds(
                                pl.multiple_of(
                                    at_ref[(head * blocks + block) * KEY_SET + j], BLK
                                ),
                                BLK,
                            ),
                            :,
                        ]
                        for j in range(KEY_SET)
                    ],
                    axis=0,
                )
            )
        for i in range(TOGETHER):
            scores.append(
                lax.dot_general(
                    q_ref[rows[i], :],
                    keys[i][:, :HEAD_DIMENSION],
                    TRANSPOSED,
                    preferred_element_type=jnp.float32,
                )
            )
        for i in range(TOGETHER):
            largest = jnp.max(scores[i], axis=-1, keepdims=True)
            weight = jnp.exp2((scores[i] - largest) * EXPONENT)
            totals.append(jnp.sum(weight, axis=-1, keepdims=True))
            weights.append(weight.astype(jnp.bfloat16))
        for i in range(TOGETHER):
            out = jnp.dot(
                weights[i], keys[i][:, HEAD_DIMENSION:], preferred_element_type=jnp.float32
            )
            o_ref[rows[i], :] = (out / totals[i]).astype(jnp.bfloat16)
        return carry

    lax.fori_loop(0, blocks // TOGETHER, step, 0)


def sparse(at, queries, sources, places, span):
    rows, width = queries.shape
    heads = width // HEAD_DIMENSION
    return pl.pallas_call(
        functools.partial(sparse_kernel, places, heads, rows // BLK),
        grid_spec=pltpu.PrefetchScalarGridSpec(
            num_scalar_prefetch=1,
            grid=(heads,),
            in_specs=[pl.BlockSpec((rows, HEAD_DIMENSION), lambda i, s: (0, i))]
            + [pl.BlockSpec(memory_space=pltpu.HBM)] * len(sources),
            out_specs=pl.BlockSpec((rows, HEAD_DIMENSION), lambda i, s: (0, i)),
            scratch_shapes=[
                pltpu.VMEM((2, span, 2 * HEAD_DIMENSION), jnp.bfloat16),
                pltpu.SemaphoreType.DMA((2,)),
            ],
        ),
        out_shape=jax.ShapeDtypeStruct(queries.shape, jnp.bfloat16),
        compiler_params=pltpu.CompilerParams(vmem_limit_bytes=48 << 20),
    )(at, queries, *sources)


def lead_kernel(places, step, head_ref, q_ref, *refs):
    sources, (o_ref, held, scores, sem) = refs[: len(places)], refs[len(places) :]
    copies = column_copies(sources, places, head_ref[0], held, sem.at[0])
    for copy in copies:
        copy.start()
    for copy in copies:
        copy.wait()
    q = q_ref[...]
    spans = [pl.ds(i, step) for i in range(0, held.shape[0], step)]
    for span in spans:
        scores[:, span] = lax.dot_general(
            q, held[span, :HEAD_DIMENSION], TRANSPOSED, preferred_element_type=jnp.float32
        )
    largest = jnp.max(scores[...], axis=-1, keepdims=True)
    total = jnp.zeros_like(largest)
    out = jnp.zeros(o_ref.shape, jnp.float32)
    for span in spans:
        weight = jnp.exp2((scores[:, span] - largest) * EXPONENT)
        total += jnp.sum(weight, axis=-1, keepdims=True)
        out += jnp.dot(
            weight.astype(jnp.bfloat16),
            held[span, HEAD_DIMENSION:],
            preferred_element_type=jnp.float32,
        )
    o_ref[...] = (out / total).astype(jnp.bfloat16)


def lead(head, queries, sources, places, span):
    return pl.pallas_call(
        functools.partial(lead_kernel, places, 1024),
        grid_spec=pltpu.PrefetchScalarGridSpec(
            num_scalar_prefetch=1,
            grid=(1,),
            in_specs=[pl.BlockSpec(queries.shape, lambda i, s: (0, 0))]
            + [pl.BlockSpec(memory_space=pltpu.HBM)] * len(sources),
            out_specs=pl.BlockSpec(queries.shape, lambda i, s: (0, 0)),
            scratch_shapes=[
                pltpu.VMEM((span, 2 * HEAD_DIMENSION), jnp.bfloat16),
                pltpu.VMEM((queries.shape[0], span), jnp.float32),
                pltpu.SemaphoreType.DMA((1,)),
            ],
        ),
        out_shape=jax.ShapeDtypeStruct(queries.shape, jnp.bfloat16),
        compiler_params=pltpu.CompilerParams(vmem_limit_bytes=48 << 20),
    )(head, queries, *sources)


def crossed(cells, bit, count):
    return lax.ppermute(cells, "ctx", [(i, i ^ bit) for i in range(count)])


def spread(own, count, turned):
    bits = [1 << i for i in range(1, count.bit_length() - 1)]
    held = {0: own}
    for bit in (bits[::-1] if turned else bits) + [1]:
        held.update({run ^ bit: crossed(cells, bit, count) for run, cells in list(held.items())})
    return held


def awaited(parts):
    near = [parts[-1][run] for run in (2, 4) if run in parts[-1]] if parts else []
    return near + ([cells for run, cells in parts[-2].items() if run] if len(parts) > 1 else [])


def from_first(cells, count):
    me = lax.axis_index("ctx")
    knows = [0]
    for bit in [1 << i for i in range(1, count.bit_length() - 1)] + [1]:
        got = lax.ppermute(cells, "ctx", [(i, i ^ bit) for i in knows])
        cells = jnp.where((me & bit) != 0, got, cells)
        knows = knows + [i ^ bit for i in knows]
    return cells


def per_device(tokens, proj_weight, partner_shard, partner_block):
    rows = tokens.shape[0]
    depth, heads, _ = proj_weight.shape
    blocks = rows // BLK
    count = lax.axis_size("ctx")
    me = lax.axis_index("ctx")
    span = rows * count
    weight = proj_weight.reshape(depth, heads * 3 * HEAD_DIMENSION)

    mine = me * blocks + jnp.arange(blocks)
    near = (mine[:, None] + jnp.array([-1, 0, 1])) % (count * blocks)
    fixed = jnp.concatenate(
        [near, jnp.broadcast_to(jnp.arange(GLOB)[None], (blocks, GLOB))], axis=1
    )
    partners = lax.dynamic_slice_in_dim(partner_shard * blocks + partner_block, me * blocks, blocks, 1)
    key_set = jnp.concatenate(
        [jnp.broadcast_to(fixed[None], (heads, blocks, 3 + GLOB)), partners], axis=2
    ).astype(jnp.int32)
    at = (((key_set // blocks) ^ me) * rows + (key_set % blocks) * BLK).astype(jnp.int32)

    sources, places = [], []
    queries, start = None, 0
    parts = []
    for part, share in enumerate(PARTS):
        size = rows * share // sum(PARTS)
        x = lax.all_gather(
            lax.slice_in_dim(tokens, start, start + size), "head", axis=1, tiled=True
        )
        queries, keyval = project(
            x, weight, queries, start, rows, awaited(parts)
        )
        if part == 0:
            lead_queries = from_first(queries[:LEAD], count)
        parts.append(spread(keyval, count, part % 2 == 1))
        for run, cells in parts[-1].items():
            sources.append(cells)
            places.append(run * rows + start)
        start += size

    share = heads * LEAD // count
    head = (me * share) // LEAD
    mine = lax.dynamic_slice(
        lead_queries, ((me * share) % LEAD, head * HEAD_DIMENSION), (share, HEAD_DIMENSION)
    )
    lead_out = lead(head.astype(jnp.int32).reshape(1), mine, sources, places, span)
    lead_out = lax.all_gather(lead_out, "ctx", axis=0, tiled=True)
    lead_out = jnp.transpose(lead_out.reshape(heads, LEAD, HEAD_DIMENSION), (1, 0, 2))
    out = sparse(at.reshape(-1), queries, sources, places, span)
    out = out.reshape(rows, heads, HEAD_DIMENSION)
    first = jnp.where(me == 0, lead_out, out[:LEAD])
    return jnp.concatenate([first, out[LEAD:]], axis=0)


def solution(mesh):
    in_specs = (
        P("ctx", "head"),
        P(None, "head", None),
        P("head", None, None),
        P("head", None, None),
    )
    out_specs = P("ctx", "head", None)
    return jax.shard_map(
        per_device, mesh=mesh, in_specs=in_specs, out_specs=out_specs, check_vma=False
    )
```

```python
import functools

import jax
import jax.numpy as jnp
from jax import lax
from jax.experimental import pallas as pl
from jax.experimental.pallas import tpu as pltpu
from jax.sharding import PartitionSpec as P

HEAD_DIMENSION = 128
BLK = 64
GLOB = 2
RAND = 3
KEY_SET = 3 + GLOB + RAND
LEAD = GLOB * BLK
EXPONENT = HEAD_DIMENSION ** (-0.5) * 1.4426950408889634
PARTS = (4, 4, 4, 4)
PERMUTED = (False, False, False, False)
TOGETHER = 8
PER = 2
VMEM = 60 << 20
TRANSPOSED = (((1,), (1,)), ((), ()))


def project_kernel(line, count, start, *refs):
    pieces, refs = refs[:count], refs[count:]
    w_ref, (q_ref, kv_ref, x_ref, hold_ref, sem) = refs[0], refs[-5:]
    step = pl.program_id(0)
    rows = x_ref.shape[0]

    @pl.when(step == 0)
    def _():
        def fetch(piece, column):
            width = piece.shape[1]
            at = pl.multiple_of(column * width, 128)
            return pltpu.make_async_copy(piece, x_ref.at[:, pl.ds(at, width)], sem)

        if not line:
            copies = [(True, fetch(pieces[0], 0))]
        else:
            z = lax.axis_index("head")
            own, below, above, two, far = pieces
            copies = [
                (True, fetch(own, z)),
                (True, fetch(two, lax.rem(z + 2, 4))),
                (z < 3, fetch(above, lax.min(z + 1, 3))),
                (z > 0, fetch(below, lax.max(z - 1, 0))),
                (jnp.logical_or(z == 0, z == 3), fetch(far, jnp.where(z == 0, 3, 0))),
            ]
        for here, copy in copies:
            pl.when(here)(copy.start)
        for here, copy in copies:
            pl.when(here)(copy.wait)

    out = jnp.dot(x_ref[...], w_ref[...], preferred_element_type=jnp.float32).astype(jnp.bfloat16)
    per = out.shape[1] // (3 * HEAD_DIMENSION)
    for i in range(per):
        at = i * 3 * HEAD_DIMENSION
        hold_ref[step, :, i * HEAD_DIMENSION : (i + 1) * HEAD_DIMENSION] = out[
            :, at : at + HEAD_DIMENSION
        ]
        kv_ref[:, 2 * i * HEAD_DIMENSION : 2 * (i + 1) * HEAD_DIMENSION] = out[
            :, at + HEAD_DIMENSION : at + 3 * HEAD_DIMENSION
        ]
    width = per * HEAD_DIMENSION
    copies = [
        pltpu.make_async_copy(
            hold_ref.at[i], q_ref.at[pl.ds(start, rows), pl.ds(i * width, width)], sem
        )
        for i in range(hold_ref.shape[0])
    ]
    for i, copy in enumerate(copies):
        pl.when(step == i)(copy.start)

    @pl.when(step == len(copies) - 1)
    def _():
        for copy in copies:
            copy.wait()


def project(pieces, weight, queries, start, total, after):
    rows = pieces[0].shape[0]
    depth = weight.shape[0]
    heads = weight.shape[1] // (3 * HEAD_DIMENSION)
    per = PER
    given = () if queries is None else (queries,)
    anywhere = pl.BlockSpec(memory_space=pl.ANY)
    return pl.pallas_call(
        functools.partial(project_kernel, len(pieces) > 1, len(pieces), start),
        grid=(heads // per,),
        in_specs=[anywhere] * len(pieces)
        + [pl.BlockSpec((depth, per * 3 * HEAD_DIMENSION), lambda i: (0, i))]
        + [anywhere] * (len(given) + len(after)),
        out_specs=[anywhere, pl.BlockSpec((rows, per * 2 * HEAD_DIMENSION), lambda i: (0, i))],
        out_shape=[
            jax.ShapeDtypeStruct((total, heads * HEAD_DIMENSION), jnp.bfloat16),
            jax.ShapeDtypeStruct((rows, heads * 2 * HEAD_DIMENSION), jnp.bfloat16),
        ],
        scratch_shapes=[
            pltpu.VMEM((rows, depth), jnp.bfloat16),
            pltpu.VMEM((heads // per, rows, per * HEAD_DIMENSION), jnp.bfloat16),
            pltpu.SemaphoreType.DMA(()),
        ],
        input_output_aliases={len(pieces) + 1: 0} if given else {},
        compiler_params=pltpu.CompilerParams(vmem_limit_bytes=VMEM),
    )(*pieces, weight, *given, *after)


def column_copies(sources, places, head, target, sem):
    at = pl.multiple_of(head * 2 * HEAD_DIMENSION, 2 * HEAD_DIMENSION)
    return [
        pltpu.make_async_copy(
            ref.at[:, pl.ds(at, 2 * HEAD_DIMENSION)], target.at[pl.ds(place, ref.shape[0]), :], sem
        )
        for ref, place in zip(sources, places)
    ]


def sparse_kernel(places, heads, blocks, at_ref, q_ref, *refs):
    sources, (o_ref, held, sem) = refs[: len(places)], refs[-3:]
    head = pl.program_id(0)
    slot = lax.rem(head, 2)

    def copies(which, into):
        return column_copies(sources, places, which, held.at[into], sem.at[into])

    @pl.when(head == 0)
    def _():
        for copy in copies(head, slot):
            copy.start()

    @pl.when(head + 1 < heads)
    def _():
        for copy in copies(head + 1, 1 - slot):
            copy.start()

    for copy in copies(head, slot):
        copy.wait()

    def step(group, carry):
        rows, keys, scores, weights, totals = [], [], [], [], []
        for i in range(TOGETHER):
            block = group * TOGETHER + i
            rows.append(pl.ds(pl.multiple_of(block * BLK, BLK), BLK))
            keys.append(
                jnp.concatenate(
                    [
                        held[
                            slot,
                            pl.ds(
                                pl.multiple_of(
                                    at_ref[(head * blocks + block) * KEY_SET + j], BLK
                                ),
                                BLK,
                            ),
                            :,
                        ]
                        for j in range(KEY_SET)
                    ],
                    axis=0,
                )
            )
        for i in range(TOGETHER):
            scores.append(
                lax.dot_general(
                    q_ref[rows[i], :],
                    keys[i][:, :HEAD_DIMENSION],
                    TRANSPOSED,
                    preferred_element_type=jnp.float32,
                )
            )
        for i in range(TOGETHER):
            largest = jnp.max(scores[i], axis=-1, keepdims=True)
            weight = jnp.exp2((scores[i] - largest) * EXPONENT)
            totals.append(jnp.sum(weight, axis=-1, keepdims=True))
            weights.append(weight.astype(jnp.bfloat16))
        for i in range(TOGETHER):
            out = jnp.dot(
                weights[i], keys[i][:, HEAD_DIMENSION:], preferred_element_type=jnp.float32
            )
            o_ref[rows[i], :] = (out / totals[i]).astype(jnp.bfloat16)
        return carry

    lax.fori_loop(0, blocks // TOGETHER, step, 0)


def sparse(at, queries, sources, places, span, after):
    rows, width = queries.shape
    heads = width // HEAD_DIMENSION
    return pl.pallas_call(
        functools.partial(sparse_kernel, places, heads, rows // BLK),
        grid_spec=pltpu.PrefetchScalarGridSpec(
            num_scalar_prefetch=1,
            grid=(heads,),
            in_specs=[pl.BlockSpec((rows, HEAD_DIMENSION), lambda i, s: (0, i))]
            + [pl.BlockSpec(memory_space=pl.ANY)] * (len(sources) + len(after)),
            out_specs=pl.BlockSpec((rows, HEAD_DIMENSION), lambda i, s: (0, i)),
            scratch_shapes=[
                pltpu.VMEM((2, span, 2 * HEAD_DIMENSION), jnp.bfloat16),
                pltpu.SemaphoreType.DMA((2,)),
            ],
        ),
        out_shape=jax.ShapeDtypeStruct(queries.shape, jnp.bfloat16),
        compiler_params=pltpu.CompilerParams(vmem_limit_bytes=VMEM),
    )(at, queries, *sources, *after)


def lead_kernel(places, step, heads, fresh, last, first_ref, q_ref, *refs):
    sources, refs = refs[: len(places)], refs[len(places) :]
    if not fresh:
        given, refs = refs[:3], refs[3:]
    outs, (held, sem) = refs[:-2], refs[-2:]
    head = pl.program_id(0)
    slot = lax.rem(head, 2)

    def copies(which, into):
        return column_copies(sources, places, first_ref[0] + which, held.at[into], sem.at[into])

    @pl.when(head == 0)
    def _():
        for copy in copies(head, slot):
            copy.start()

    @pl.when(head + 1 < heads)
    def _():
        for copy in copies(head + 1, 1 - slot):
            copy.start()

    for copy in copies(head, slot):
        copy.wait()
    q = q_ref[...]
    spans = [pl.ds(i, step) for i in range(0, held.shape[1], step)]
    scores = [
        lax.dot_general(
            q, held[slot, span, :HEAD_DIMENSION], TRANSPOSED, preferred_element_type=jnp.float32
        )
        for span in spans
    ]
    largest = functools.reduce(
        jnp.maximum, [jnp.max(part, axis=-1, keepdims=True) for part in scores]
    )
    if fresh:
        total, out = 0.0, 0.0
    else:
        largest = jnp.maximum(largest, given[0][:, :1])
        factor = jnp.exp2((given[0][:, :1] - largest) * EXPONENT)
        total, out = given[1][:, :1] * factor, given[2][...] * factor
    for span, part in zip(spans, scores):
        weight = jnp.exp2((part - largest) * EXPONENT)
        total += jnp.sum(weight, axis=-1, keepdims=True)
        out += jnp.dot(
            weight.astype(jnp.bfloat16),
            held[slot, span, HEAD_DIMENSION:],
            preferred_element_type=jnp.float32,
        )
    if last:
        outs[0][...] = (out / total).astype(jnp.bfloat16)
    else:
        outs[0][...] = jnp.broadcast_to(largest, outs[0].shape)
        outs[1][...] = jnp.broadcast_to(total, outs[1].shape)
        outs[2][...] = out


def lead(first, queries, sources, places, span, given, last):
    rows, width = queries.shape
    heads = width // HEAD_DIMENSION
    step = min(span, 1024)
    assert span % step == 0
    block = pl.BlockSpec((rows, HEAD_DIMENSION), lambda i, s: (0, i))
    state = [jax.ShapeDtypeStruct(queries.shape, jnp.float32)] * 3
    return pl.pallas_call(
        functools.partial(lead_kernel, places, step, heads, not given, last),
        grid_spec=pltpu.PrefetchScalarGridSpec(
            num_scalar_prefetch=1,
            grid=(heads,),
            in_specs=[block]
            + [pl.BlockSpec(memory_space=pl.ANY)] * len(sources)
            + [block] * len(given),
            out_specs=block if last else [block] * 3,
            scratch_shapes=[
                pltpu.VMEM((2, span, 2 * HEAD_DIMENSION), jnp.bfloat16),
                pltpu.SemaphoreType.DMA((2,)),
            ],
        ),
        out_shape=jax.ShapeDtypeStruct(queries.shape, jnp.bfloat16) if last else state,
        compiler_params=pltpu.CompilerParams(vmem_limit_bytes=VMEM),
    )(first, queries, *sources, *given)


def crossed(cells, bit, count):
    return lax.ppermute(cells, "ctx", [(i, i ^ bit) for i in range(count)])


def halves(cells):
    half = cells.shape[0] // 2
    return cells[:half], cells[half:]


def spread(own, count, ready=(), before=()):
    own = after(own, *ready) if ready else own
    bits = [1 << i for i in range(1, count.bit_length() - 1)]
    last, other = bits[-1], bits[-2]
    held = [(0, 0, own)]
    for bit in bits[:-2]:
        held += [(run ^ bit, at, crossed(cells, bit, count)) for run, at, cells in held]
    by_other = [(run ^ other, at, crossed(cells, other, count)) for run, at, cells in held]
    by_last = [(run ^ last, at, crossed(cells, last, count)) for run, at, cells in held]
    both = []
    for (run, at, cells), (run_too, _, cells_too) in zip(by_other, by_last):
        one, two = halves(cells)[0], halves(cells_too)[1]
        if before:
            one, two = after(one, *before), after(two, *before)
        both.append((run ^ last, at, crossed(one, last, count)))
        both.append((run_too ^ other, at + cells.shape[0] // 2, crossed(two, other, count)))
    held = held + by_other + by_last + both
    near = [cells for _, _, cells in by_other + by_last]
    far = [cells for _, _, cells in both]
    held += [(run ^ 1, at, crossed(cells, 1, count)) for run, at, cells in held]
    return held, near, far


def awaited(parts):
    near = parts[-1][1] if parts else []
    return near + ([cells for run, _, cells in parts[-2][0] if run] if len(parts) > 1 else [])


def after(cells, *others):
    in_hbm = pl.BlockSpec(memory_space=pl.ANY)
    return pl.pallas_call(
        lambda *refs: None,
        in_specs=[in_hbm] * (1 + len(others)),
        out_specs=in_hbm,
        out_shape=jax.ShapeDtypeStruct(cells.shape, cells.dtype),
        input_output_aliases={0: 0},
    )(cells, *others)


def gather_features(tokens, weight, sizes):
    found, start, two = [], 0, None
    for part, size in enumerate(sizes):
        own = lax.slice_in_dim(tokens, start, start + size)
        if PERMUTED[part] and lax.axis_size("head") == 4:
            two = lax.ppermute(own, "head", [(2, 0), (3, 1), (0, 2), (1, 3)])
            above = lax.ppermute(own, "head", [(1, 0), (2, 1), (3, 2)])
            below = lax.ppermute(own, "head", [(0, 1), (1, 2), (2, 3)])
            two = after(two, weight)
            far = lax.ppermute(two, "head", [(1, 0), (2, 3)])
            found.append((own, below, above, two, far))
        else:
            own = own if two is None else after(own, two)
            found.append((lax.all_gather(own, "head", axis=1, tiled=True),))
        start += size
    return found


def per_device(tokens, proj_weight, partner_shard, partner_block):
    rows = tokens.shape[0]
    depth, heads, _ = proj_weight.shape
    blocks = rows // BLK
    count = lax.axis_size("ctx")
    me = lax.axis_index("ctx")
    span = rows * count
    weight = proj_weight.reshape(depth, heads * 3 * HEAD_DIMENSION)

    mine = me * blocks + jnp.arange(blocks)
    near = (mine[:, None] + jnp.array([-1, 0, 1])) % (count * blocks)
    fixed = jnp.concatenate(
        [near, jnp.broadcast_to(jnp.arange(GLOB)[None], (blocks, GLOB))], axis=1
    )
    partners = lax.dynamic_slice_in_dim(partner_shard * blocks + partner_block, me * blocks, blocks, 1)
    key_set = jnp.concatenate(
        [jnp.broadcast_to(fixed[None], (heads, blocks, 3 + GLOB)), partners], axis=2
    ).astype(jnp.int32)
    at = (((key_set // blocks) ^ me) * rows + (key_set % blocks) * BLK).astype(jnp.int32)

    parts, held, given, lead_queries = [], [], (), None
    queries, start = None, 0
    sizes = [rows * share // sum(PARTS) for share in PARTS]
    half = heads // 2 * HEAD_DIMENSION
    first = jnp.where(me == 1, heads // 2, 0).astype(jnp.int32).reshape(1)

    def placed(which):
        sources, places, start = [], [], 0
        for part in which:
            for run, at_row, cells in parts[part][0]:
                sources.append(cells)
                places.append(start + run * sizes[part] + at_row)
            start += sizes[part] * count
        return sources, places, start

    def at_home():
        sources, places, start = [], [], 0
        for size, part in zip(sizes, parts):
            for run, at_row, cells in part[0]:
                sources.append(cells)
                places.append(run * rows + start + at_row)
            start += size
        return sources, places, span

    at = at.reshape(-1)
    for part, pieces in enumerate(gather_features(tokens, weight, sizes)):
        queries, keyval = project(pieces, weight, queries, start, rows, awaited(parts))
        before = []
        if part == len(sizes) - 1:
            got = lax.ppermute(queries[:LEAD, half:], "ctx", [(0, 1)])
            lead_queries = jnp.where(me == 1, got, queries[:LEAD, :half])
            given = lead(first, lead_queries, *placed(range(part)), (), False)
            before = given[:1]
        parts.append(spread(keyval, count, parts[-1][2] if parts else [], before))
        start += sizes[part]

    lead_own = lead(first, lead_queries, *placed([len(sizes) - 1]), given, True)
    lead_out = jnp.concatenate([lead_own, lax.ppermute(lead_own, "ctx", [(1, 0)])], axis=1)
    out = sparse(at, queries, *at_home(), [lead_own])
    out = out.reshape(rows, heads, HEAD_DIMENSION)
    lead_out = lead_out.reshape(LEAD, heads, HEAD_DIMENSION)
    return jnp.concatenate([jnp.where(me == 0, lead_out, out[:LEAD]), out[LEAD:]], axis=0)


def solution(mesh):
    in_specs = (
        P("ctx", "head"),
        P(None, "head", None),
        P("head", None, None),
        P("head", None, None),
    )
    out_specs = P("ctx", "head", None)
    return jax.shard_map(
        per_device, mesh=mesh, in_specs=in_specs, out_specs=out_specs, check_vma=False
    )
```

```python
import functools
import math

import jax
import jax.numpy as jnp
from jax import lax
from jax.experimental import pallas as pl
from jax.experimental.pallas import tpu as pltpu
from jax.sharding import PartitionSpec as P

HEAD_DIMENSION = 128
BLK = 64
GLOB = 2
RAND = 3
KEY_SET = 3 + GLOB + RAND
LEAD = GLOB * BLK
EXPONENT = HEAD_DIMENSION ** (-0.5) * 1.4426950408889634
PARTS = (4, 4, 4, 4)
GROUPS = (0, 1, 2, 3)
TOGETHER = 16
PER = 2
VMEM = 60 << 20
TRANSPOSED = (((1,), (1,)), ((), ()))


def project_kernel(start, x_ref, w_ref, *refs):
    q_ref, kv_ref, hold_ref, sem = refs[-4:]
    step = pl.program_id(0)
    rows = x_ref.shape[0]
    out = jnp.dot(x_ref[...], w_ref[...], preferred_element_type=jnp.float32).astype(jnp.bfloat16)
    per = out.shape[1] // (3 * HEAD_DIMENSION)
    for i in range(per):
        at = i * 3 * HEAD_DIMENSION
        hold_ref[step, :, i * HEAD_DIMENSION : (i + 1) * HEAD_DIMENSION] = out[
            :, at : at + HEAD_DIMENSION
        ]
        kv_ref[:, 2 * i * HEAD_DIMENSION : 2 * (i + 1) * HEAD_DIMENSION] = out[
            :, at + HEAD_DIMENSION : at + 3 * HEAD_DIMENSION
        ]
    width = per * HEAD_DIMENSION
    copies = [
        pltpu.make_async_copy(
            hold_ref.at[i], q_ref.at[pl.ds(start, rows), pl.ds(i * width, width)], sem
        )
        for i in range(hold_ref.shape[0])
    ]
    for i, copy in enumerate(copies):
        pl.when(step == i)(copy.start)

    @pl.when(step == len(copies) - 1)
    def _():
        for copy in copies:
            copy.wait()


def project(x, begin, rows, weight, queries, start, total, after):
    depth = x.shape[1]
    assert begin % rows == 0
    heads = weight.shape[1] // (3 * HEAD_DIMENSION)
    per = PER
    given = () if queries is None else (queries,)
    anywhere = pl.BlockSpec(memory_space=pl.ANY)
    return pl.pallas_call(
        functools.partial(project_kernel, start),
        grid=(heads // per,),
        in_specs=[
            pl.BlockSpec((rows, depth), lambda i: (begin // rows, 0)),
            pl.BlockSpec((depth, per * 3 * HEAD_DIMENSION), lambda i: (0, i)),
        ]
        + [anywhere] * (len(given) + len(after)),
        out_specs=[anywhere, pl.BlockSpec((rows, per * 2 * HEAD_DIMENSION), lambda i: (0, i))],
        out_shape=[
            jax.ShapeDtypeStruct((total, heads * HEAD_DIMENSION), jnp.bfloat16),
            jax.ShapeDtypeStruct((rows, heads * 2 * HEAD_DIMENSION), jnp.bfloat16),
        ],
        scratch_shapes=[
            pltpu.VMEM((heads // per, rows, per * HEAD_DIMENSION), jnp.bfloat16),
            pltpu.SemaphoreType.DMA(()),
        ],
        input_output_aliases={2: 0} if given else {},
        cost_estimate=pl.CostEstimate(
            flops=2 * rows * depth * weight.shape[1],
            bytes_accessed=2 * (rows * depth + (depth + rows) * weight.shape[1]),
            transcendentals=0,
        ),
        compiler_params=pltpu.CompilerParams(vmem_limit_bytes=VMEM),
    )(x, weight, *given, *after)


def column_copies(sources, places, head, target, sem):
    at = pl.multiple_of(head * 2 * HEAD_DIMENSION, 2 * HEAD_DIMENSION)
    return [
        pltpu.make_async_copy(
            ref.at[:, pl.ds(at, 2 * HEAD_DIMENSION)], target.at[pl.ds(place, ref.shape[0]), :], sem
        )
        for ref, place in zip(sources, places)
    ]


def sparse_kernel(places, heads, blocks, at_ref, q_ref, *refs):
    sources, (o_ref, held, sem) = refs[: len(places)], refs[-3:]
    head = pl.program_id(0)
    slot = lax.rem(head, 2)

    def copies(which, into):
        return column_copies(sources, places, which, held.at[into], sem.at[into])

    @pl.when(head == 0)
    def _():
        for copy in copies(head, slot):
            copy.start()

    @pl.when(head + 1 < heads)
    def _():
        for copy in copies(head + 1, 1 - slot):
            copy.start()

    for copy in copies(head, slot):
        copy.wait()

    def step(group, carry):
        rows, keys, scores, weights, totals = [], [], [], [], []
        for i in range(TOGETHER):
            block = group * TOGETHER + i
            rows.append(pl.ds(pl.multiple_of(block * BLK, BLK), BLK))
            keys.append(
                jnp.concatenate(
                    [
                        held[
                            slot,
                            pl.ds(
                                pl.multiple_of(
                                    at_ref[(head * blocks + block) * KEY_SET + j], BLK
                                ),
                                BLK,
                            ),
                            :,
                        ]
                        for j in range(KEY_SET)
                    ],
                    axis=0,
                )
            )
        for i in range(TOGETHER):
            scores.append(
                lax.dot_general(
                    q_ref[rows[i], :],
                    keys[i][:, :HEAD_DIMENSION],
                    TRANSPOSED,
                    preferred_element_type=jnp.float32,
                )
            )
        for i in range(TOGETHER):
            largest = jnp.max(scores[i], axis=-1, keepdims=True)
            weight = jnp.exp2((scores[i] - largest) * EXPONENT)
            totals.append(jnp.sum(weight, axis=-1, keepdims=True))
            weights.append(weight.astype(jnp.bfloat16))
        for i in range(TOGETHER):
            out = jnp.dot(
                weights[i], keys[i][:, HEAD_DIMENSION:], preferred_element_type=jnp.float32
            )
            o_ref[rows[i], :] = (out / totals[i]).astype(jnp.bfloat16)
        return carry

    lax.fori_loop(0, blocks // TOGETHER, step, 0)


def sparse(at, queries, sources, places, span, after):
    rows, width = queries.shape
    heads = width // HEAD_DIMENSION
    return pl.pallas_call(
        functools.partial(sparse_kernel, places, heads, rows // BLK),
        grid_spec=pltpu.PrefetchScalarGridSpec(
            num_scalar_prefetch=1,
            grid=(heads,),
            in_specs=[pl.BlockSpec((rows, HEAD_DIMENSION), lambda i, s: (0, i))]
            + [pl.BlockSpec(memory_space=pl.ANY)] * (len(sources) + len(after)),
            out_specs=pl.BlockSpec((rows, HEAD_DIMENSION), lambda i, s: (0, i)),
            scratch_shapes=[
                pltpu.VMEM((2, span, 2 * HEAD_DIMENSION), jnp.bfloat16),
                pltpu.SemaphoreType.DMA((2,)),
            ],
        ),
        out_shape=jax.ShapeDtypeStruct(queries.shape, jnp.bfloat16),
        cost_estimate=pl.CostEstimate(
            flops=4 * rows * heads * KEY_SET * BLK * HEAD_DIMENSION,
            bytes_accessed=4 * (span + rows) * heads * HEAD_DIMENSION,
            transcendentals=rows * heads * KEY_SET * BLK,
        ),
        compiler_params=pltpu.CompilerParams(vmem_limit_bytes=VMEM),
    )(at, queries, *sources, *after)


def lead_kernel(places, step, heads, fresh, last, first_ref, q_ref, *refs):
    sources, refs = refs[: len(places)], refs[len(places) :]
    if not fresh:
        given, refs = refs[:3], refs[3:]
    outs, (held, sem) = refs[:-2], refs[-2:]
    head = pl.program_id(0)
    slot = lax.rem(head, 2)

    def copies(which, into):
        return column_copies(sources, places, first_ref[0] + which, held.at[into], sem.at[into])

    @pl.when(head == 0)
    def _():
        for copy in copies(head, slot):
            copy.start()

    @pl.when(head + 1 < heads)
    def _():
        for copy in copies(head + 1, 1 - slot):
            copy.start()

    for copy in copies(head, slot):
        copy.wait()
    q = q_ref[...]
    spans = [pl.ds(i, step) for i in range(0, held.shape[1], step)]
    scores = [
        lax.dot_general(
            q, held[slot, span, :HEAD_DIMENSION], TRANSPOSED, preferred_element_type=jnp.float32
        )
        for span in spans
    ]
    largest = functools.reduce(
        jnp.maximum, [jnp.max(part, axis=-1, keepdims=True) for part in scores]
    )
    if fresh:
        total, out = 0.0, 0.0
    else:
        largest = jnp.maximum(largest, given[0][:, :1])
        factor = jnp.exp2((given[0][:, :1] - largest) * EXPONENT)
        total, out = given[1][:, :1] * factor, given[2][...] * factor
    for span, part in zip(spans, scores):
        weight = jnp.exp2((part - largest) * EXPONENT)
        total += jnp.sum(weight, axis=-1, keepdims=True)
        out += jnp.dot(
            weight.astype(jnp.bfloat16),
            held[slot, span, HEAD_DIMENSION:],
            preferred_element_type=jnp.float32,
        )
    if last:
        outs[0][...] = (out / total).astype(jnp.bfloat16)
    else:
        outs[0][...] = jnp.broadcast_to(largest, outs[0].shape)
        outs[1][...] = jnp.broadcast_to(total, outs[1].shape)
        outs[2][...] = out


def lead(first, queries, sources, places, span, given, last):
    rows, width = queries.shape
    heads = width // HEAD_DIMENSION
    step = math.gcd(span, 1024)
    assert span % step == 0
    block = pl.BlockSpec((rows, HEAD_DIMENSION), lambda i, s: (0, i))
    state = [jax.ShapeDtypeStruct(queries.shape, jnp.float32)] * 3
    return pl.pallas_call(
        functools.partial(lead_kernel, places, step, heads, not given, last),
        grid_spec=pltpu.PrefetchScalarGridSpec(
            num_scalar_prefetch=1,
            grid=(heads,),
            in_specs=[block]
            + [pl.BlockSpec(memory_space=pl.ANY)] * len(sources)
            + [block] * len(given),
            out_specs=block if last else [block] * 3,
            scratch_shapes=[
                pltpu.VMEM((2, span, 2 * HEAD_DIMENSION), jnp.bfloat16),
                pltpu.SemaphoreType.DMA((2,)),
            ],
        ),
        out_shape=jax.ShapeDtypeStruct(queries.shape, jnp.bfloat16) if last else state,
        cost_estimate=pl.CostEstimate(
            flops=4 * rows * width * span,
            bytes_accessed=4 * span * width,
            transcendentals=rows * heads * span,
        ),
        compiler_params=pltpu.CompilerParams(vmem_limit_bytes=VMEM),
    )(first, queries, *sources, *given)


def crossed(cells, bit, count):
    return lax.ppermute(cells, "ctx", [(i, i ^ bit) for i in range(count)])


def halves(cells):
    half = cells.shape[0] // 2
    return cells[:half], cells[half:]


def spread(own, count, ready=(), before=()):
    own = after(own, *ready) if ready else own
    bits = [1 << i for i in range(1, count.bit_length() - 1)]
    last, other = bits[-1], bits[-2]
    held = [(0, 0, own)]
    for bit in bits[:-2]:
        held += [(run ^ bit, at, crossed(cells, bit, count)) for run, at, cells in held]
    by_other = [(run ^ other, at, crossed(cells, other, count)) for run, at, cells in held]
    by_last = [(run ^ last, at, crossed(cells, last, count)) for run, at, cells in held]
    both = []
    for (run, at, cells), (run_too, _, cells_too) in zip(by_other, by_last):
        one, two = halves(cells)[0], halves(cells_too)[1]
        if before:
            one, two = after(one, *before), after(two, *before)
        both.append((run ^ last, at, crossed(one, last, count)))
        both.append((run_too ^ other, at + cells.shape[0] // 2, crossed(two, other, count)))
    held = held + by_other + by_last + both
    near = [cells for _, _, cells in by_other + by_last]
    far = [cells for _, _, cells in both]
    held += [(run ^ 1, at, crossed(cells, 1, count)) for run, at, cells in held]
    return held, near, far


def after(cells, *others):
    in_hbm = pl.BlockSpec(memory_space=pl.ANY)
    return pl.pallas_call(
        lambda *refs: None,
        in_specs=[in_hbm] * (1 + len(others)),
        out_specs=in_hbm,
        out_shape=jax.ShapeDtypeStruct(cells.shape, cells.dtype),
        input_output_aliases={0: 0},
    )(cells, *others)


def cut_kernel(start, x_ref, *refs):
    o_ref, sem = refs[-2:]
    copy = pltpu.make_async_copy(x_ref.at[pl.ds(start, o_ref.shape[0]), :], o_ref, sem)
    copy.start()
    copy.wait()


def cut(cells, start, size, after):
    anywhere = pl.BlockSpec(memory_space=pl.ANY)
    return pl.pallas_call(
        functools.partial(cut_kernel, start),
        grid=(1,),
        in_specs=[anywhere] * (1 + len(after)),
        out_specs=pl.BlockSpec((size, cells.shape[1]), lambda i: (0, 0)),
        out_shape=jax.ShapeDtypeStruct((size, cells.shape[1]), cells.dtype),
        scratch_shapes=[pltpu.SemaphoreType.DMA(())],
    )(cells, *after)


def gather_features(tokens, weight, sizes):
    found, start = [], 0
    for group in range(GROUPS[-1] + 1):
        members = [size for size, own in zip(sizes, GROUPS) if own == group]
        own = cut(tokens, start, sum(members), [weight] if start else [])
        full = lax.all_gather(own, "head", axis=1, tiled=True)
        found += [(full, sum(members[:i])) for i in range(len(members))]
        start += sum(members)
    return found


def per_device(tokens, proj_weight, partner_shard, partner_block):
    rows = tokens.shape[0]
    depth, heads, _ = proj_weight.shape
    blocks = rows // BLK
    count = lax.axis_size("ctx")
    me = lax.axis_index("ctx")
    span = rows * count
    weight = proj_weight.reshape(depth, heads * 3 * HEAD_DIMENSION)

    mine = me * blocks + jnp.arange(blocks)
    near = (mine[:, None] + jnp.array([-1, 0, 1])) % (count * blocks)
    fixed = jnp.concatenate(
        [near, jnp.broadcast_to(jnp.arange(GLOB)[None], (blocks, GLOB))], axis=1
    )
    partners = lax.dynamic_slice_in_dim(partner_shard * blocks + partner_block, me * blocks, blocks, 1)
    key_set = jnp.concatenate(
        [jnp.broadcast_to(fixed[None], (heads, blocks, 3 + GLOB)), partners], axis=2
    ).astype(jnp.int32)
    at = (((key_set // blocks) ^ me) * rows + (key_set % blocks) * BLK).astype(jnp.int32)

    parts, held, given, lead_queries = [], [], (), None
    queries, start = None, 0
    sizes = [rows * share // sum(PARTS) for share in PARTS]
    half = heads // 2 * HEAD_DIMENSION
    first = jnp.where(me == 1, heads // 2, 0).astype(jnp.int32).reshape(1)

    def placed(which):
        sources, places, start = [], [], 0
        for part in which:
            for run, at_row, cells in parts[part][0]:
                sources.append(cells)
                places.append(start + run * sizes[part] + at_row)
            start += sizes[part] * count
        return sources, places, start

    def at_home():
        sources, places, start = [], [], 0
        for size, part in zip(sizes, parts):
            for run, at_row, cells in part[0]:
                sources.append(cells)
                places.append(run * rows + start + at_row)
            start += size
        return sources, places, span

    at = at.reshape(-1)
    for part, (x, begin) in enumerate(gather_features(tokens, weight, sizes)):
        fresh = part == 0 or GROUPS[part] > GROUPS[part - 1]
        near, far = parts[-1][1:] if parts else ([], [])
        settled = [cells for run, _, cells in parts[-2][0] if run] if part > 1 else []
        queries, keyval = project(
            x, begin, sizes[part], weight, queries, start, rows, settled + (near if fresh else [])
        )
        ready, before = (far, []) if fresh else (near, far)
        if part == len(sizes) - 1:
            got = lax.ppermute(queries[:LEAD, half:], "ctx", [(0, 1)])
            lead_queries = jnp.where(me == 1, got, queries[:LEAD, :half])
            given = lead(first, lead_queries, *placed(range(part)), (), False)
            before = [given[0]] + before
        parts.append(spread(keyval, count, ready, before))
        start += sizes[part]

    lead_own = lead(first, lead_queries, *placed([len(sizes) - 1]), given, True)
    lead_out = jnp.concatenate([lead_own, lax.ppermute(lead_own, "ctx", [(1, 0)])], axis=1)
    out = sparse(at, queries, *at_home(), [lead_own])
    out = out.reshape(rows, heads, HEAD_DIMENSION)
    lead_out = lead_out.reshape(LEAD, heads, HEAD_DIMENSION)
    return jnp.concatenate([jnp.where(me == 0, lead_out, out[:LEAD]), out[LEAD:]], axis=0)


def solution(mesh):
    in_specs = (
        P("ctx", "head"),
        P(None, "head", None),
        P("head", None, None),
        P("head", None, None),
    )
    out_specs = P("ctx", "head", None)
    return jax.shard_map(
        per_device, mesh=mesh, in_specs=in_specs, out_specs=out_specs, check_vma=False
    )
```

```python
import functools
import math

import jax
import jax.numpy as jnp
from jax import lax
from jax.experimental import pallas as pl
from jax.experimental.pallas import tpu as pltpu
from jax.sharding import PartitionSpec as P

HEAD_DIMENSION = 128
BLK = 64
GLOB = 2
RAND = 3
KEY_SET = 3 + GLOB + RAND
LEAD = GLOB * BLK
EXPONENT = HEAD_DIMENSION ** (-0.5) * 1.4426950408889634
PARTS = (4, 4, 4, 4)
GROUPS = (0, 1, 2, 3)
TOGETHER = 16
COLUMNS = 512
VMEM = 60 << 20
TRANSPOSED = (((1,), (1,)), ((), ()))


def project_kernel(x_ref, w_ref, *refs):
    o_ref = refs[-1]
    out = jnp.dot(x_ref[...], w_ref[...], preferred_element_type=jnp.float32)
    o_ref[...] = out.astype(jnp.bfloat16)


def project(x, weight, into, start, total, after):
    rows, depth = x.shape
    columns = weight.shape[1]
    wide = min(COLUMNS, columns)
    assert start % rows == 0
    given = () if into is None else (into,)
    anywhere = pl.BlockSpec(memory_space=pl.ANY)
    return pl.pallas_call(
        project_kernel,
        grid=(columns // wide,),
        in_specs=[
            pl.BlockSpec((rows, depth), lambda i: (0, 0)),
            pl.BlockSpec((depth, wide), lambda i: (0, i)),
        ]
        + [anywhere] * (len(given) + len(after)),
        out_specs=pl.BlockSpec((rows, wide), lambda i: (start // rows, i)),
        out_shape=jax.ShapeDtypeStruct((total, columns), jnp.bfloat16),
        input_output_aliases={2: 0} if given else {},
        cost_estimate=pl.CostEstimate(
            flops=2 * rows * depth * columns,
            bytes_accessed=2 * (rows * depth + (depth + rows) * columns),
            transcendentals=0,
        ),
        compiler_params=pltpu.CompilerParams(vmem_limit_bytes=VMEM),
    )(x, weight, *given, *after)


def column_copies(sources, places, head, target, sem):
    at = pl.multiple_of(head * 2 * HEAD_DIMENSION, 2 * HEAD_DIMENSION)
    return [
        pltpu.make_async_copy(
            ref.at[:, pl.ds(at, 2 * HEAD_DIMENSION)], target.at[pl.ds(place, ref.shape[0]), :], sem
        )
        for ref, place in zip(sources, places)
    ]


def sparse_kernel(places, heads, blocks, at_ref, q_ref, *refs):
    sources, (o_ref, held, sem) = refs[: len(places)], refs[-3:]
    head = pl.program_id(0)
    slot = lax.rem(head, 2)

    def copies(which, into):
        return column_copies(sources, places, which, held.at[into], sem.at[into])

    @pl.when(head == 0)
    def _():
        for copy in copies(head, slot):
            copy.start()

    @pl.when(head + 1 < heads)
    def _():
        for copy in copies(head + 1, 1 - slot):
            copy.start()

    for copy in copies(head, slot):
        copy.wait()

    def step(group, carry):
        rows, keys, scores, weights, totals = [], [], [], [], []
        for i in range(TOGETHER):
            block = group * TOGETHER + i
            rows.append(pl.ds(pl.multiple_of(block * BLK, BLK), BLK))
            keys.append(
                jnp.concatenate(
                    [
                        held[
                            slot,
                            pl.ds(
                                pl.multiple_of(
                                    at_ref[(head * blocks + block) * KEY_SET + j], BLK
                                ),
                                BLK,
                            ),
                            :,
                        ]
                        for j in range(KEY_SET)
                    ],
                    axis=0,
                )
            )
        for i in range(TOGETHER):
            scores.append(
                lax.dot_general(
                    q_ref[rows[i], :],
                    keys[i][:, :HEAD_DIMENSION],
                    TRANSPOSED,
                    preferred_element_type=jnp.float32,
                )
            )
        for i in range(TOGETHER):
            largest = jnp.max(scores[i], axis=-1, keepdims=True)
            weight = jnp.exp2((scores[i] - largest) * EXPONENT)
            totals.append(jnp.sum(weight, axis=-1, keepdims=True))
            weights.append(weight.astype(jnp.bfloat16))
        for i in range(TOGETHER):
            out = jnp.dot(
                weights[i], keys[i][:, HEAD_DIMENSION:], preferred_element_type=jnp.float32
            )
            o_ref[rows[i], :] = (out / totals[i]).astype(jnp.bfloat16)
        return carry

    lax.fori_loop(0, blocks // TOGETHER, step, 0)


def sparse(at, queries, sources, places, span, after):
    rows, width = queries.shape
    heads = width // HEAD_DIMENSION
    return pl.pallas_call(
        functools.partial(sparse_kernel, places, heads, rows // BLK),
        grid_spec=pltpu.PrefetchScalarGridSpec(
            num_scalar_prefetch=1,
            grid=(heads,),
            in_specs=[pl.BlockSpec((rows, HEAD_DIMENSION), lambda i, s: (0, i))]
            + [pl.BlockSpec(memory_space=pl.ANY)] * (len(sources) + len(after)),
            out_specs=pl.BlockSpec((rows, HEAD_DIMENSION), lambda i, s: (0, i)),
            scratch_shapes=[
                pltpu.VMEM((2, span, 2 * HEAD_DIMENSION), jnp.bfloat16),
                pltpu.SemaphoreType.DMA((2,)),
            ],
        ),
        out_shape=jax.ShapeDtypeStruct(queries.shape, jnp.bfloat16),
        cost_estimate=pl.CostEstimate(
            flops=4 * rows * heads * KEY_SET * BLK * HEAD_DIMENSION,
            bytes_accessed=4 * (span + rows) * heads * HEAD_DIMENSION,
            transcendentals=rows * heads * KEY_SET * BLK,
        ),
        compiler_params=pltpu.CompilerParams(vmem_limit_bytes=VMEM),
    )(at, queries, *sources, *after)


def lead_kernel(places, step, heads, fresh, last, first_ref, q_ref, *refs):
    sources, refs = refs[: len(places)], refs[len(places) :]
    if not fresh:
        given, refs = refs[:3], refs[3:]
    outs, (held, sem) = refs[:-2], refs[-2:]
    head = pl.program_id(0)
    slot = lax.rem(head, 2)

    def copies(which, into):
        return column_copies(sources, places, first_ref[0] + which, held.at[into], sem.at[into])

    @pl.when(head == 0)
    def _():
        for copy in copies(head, slot):
            copy.start()

    @pl.when(head + 1 < heads)
    def _():
        for copy in copies(head + 1, 1 - slot):
            copy.start()

    for copy in copies(head, slot):
        copy.wait()
    q = q_ref[...]
    spans = [pl.ds(i, step) for i in range(0, held.shape[1], step)]
    scores = [
        lax.dot_general(
            q, held[slot, span, :HEAD_DIMENSION], TRANSPOSED, preferred_element_type=jnp.float32
        )
        for span in spans
    ]
    largest = functools.reduce(
        jnp.maximum, [jnp.max(part, axis=-1, keepdims=True) for part in scores]
    )
    if fresh:
        total, out = 0.0, 0.0
    else:
        largest = jnp.maximum(largest, given[0][:, :1])
        factor = jnp.exp2((given[0][:, :1] - largest) * EXPONENT)
        total, out = given[1][:, :1] * factor, given[2][...] * factor
    for span, part in zip(spans, scores):
        weight = jnp.exp2((part - largest) * EXPONENT)
        total += jnp.sum(weight, axis=-1, keepdims=True)
        out += jnp.dot(
            weight.astype(jnp.bfloat16),
            held[slot, span, HEAD_DIMENSION:],
            preferred_element_type=jnp.float32,
        )
    if last:
        outs[0][...] = (out / total).astype(jnp.bfloat16)
    else:
        outs[0][...] = jnp.broadcast_to(largest, outs[0].shape)
        outs[1][...] = jnp.broadcast_to(total, outs[1].shape)
        outs[2][...] = out


def lead(first, queries, sources, places, span, given, last):
    rows, width = queries.shape
    heads = width // HEAD_DIMENSION
    step = math.gcd(span, 1024)
    assert span % step == 0
    block = pl.BlockSpec((rows, HEAD_DIMENSION), lambda i, s: (0, i))
    state = [jax.ShapeDtypeStruct(queries.shape, jnp.float32)] * 3
    return pl.pallas_call(
        functools.partial(lead_kernel, places, step, heads, not given, last),
        grid_spec=pltpu.PrefetchScalarGridSpec(
            num_scalar_prefetch=1,
            grid=(heads,),
            in_specs=[block]
            + [pl.BlockSpec(memory_space=pl.ANY)] * len(sources)
            + [block] * len(given),
            out_specs=block if last else [block] * 3,
            scratch_shapes=[
                pltpu.VMEM((2, span, 2 * HEAD_DIMENSION), jnp.bfloat16),
                pltpu.SemaphoreType.DMA((2,)),
            ],
        ),
        out_shape=jax.ShapeDtypeStruct(queries.shape, jnp.bfloat16) if last else state,
        cost_estimate=pl.CostEstimate(
            flops=4 * rows * width * span,
            bytes_accessed=4 * span * width,
            transcendentals=rows * heads * span,
        ),
        compiler_params=pltpu.CompilerParams(vmem_limit_bytes=VMEM),
    )(first, queries, *sources, *given)


def crossed(cells, bit, count):
    return lax.ppermute(cells, "ctx", [(i, i ^ bit) for i in range(count)])


def halves(cells):
    half = cells.shape[0] // 2
    return cells[:half], cells[half:]


def spread(own, count, ready=(), before=()):
    own = after(own, *ready) if ready else own
    bits = [1 << i for i in range(1, count.bit_length() - 1)]
    last, other = bits[-1], bits[-2]
    held = [(0, 0, own)]
    for bit in bits[:-2]:
        held += [(run ^ bit, at, crossed(cells, bit, count)) for run, at, cells in held]
    by_other = [(run ^ other, at, crossed(cells, other, count)) for run, at, cells in held]
    by_last = [(run ^ last, at, crossed(cells, last, count)) for run, at, cells in held]
    both = []
    for (run, at, cells), (run_too, _, cells_too) in zip(by_other, by_last):
        one, two = halves(cells)[0], halves(cells_too)[1]
        if before:
            one, two = after(one, *before), after(two, *before)
        both.append((run ^ last, at, crossed(one, last, count)))
        both.append((run_too ^ other, at + cells.shape[0] // 2, crossed(two, other, count)))
    held = held + by_other + by_last + both
    near = [cells for _, _, cells in by_other + by_last]
    far = [cells for _, _, cells in both]
    held += [(run ^ 1, at, crossed(cells, 1, count)) for run, at, cells in held]
    return held, near, far


def after(cells, *others):
    in_hbm = pl.BlockSpec(memory_space=pl.ANY)
    return pl.pallas_call(
        lambda *refs: None,
        in_specs=[in_hbm] * (1 + len(others)),
        out_specs=in_hbm,
        out_shape=jax.ShapeDtypeStruct(cells.shape, cells.dtype),
        input_output_aliases={0: 0},
    )(cells, *others)


def cut_kernel(start, x_ref, *refs):
    o_ref, sem = refs[-2:]
    copy = pltpu.make_async_copy(x_ref.at[pl.ds(start, o_ref.shape[0]), :], o_ref, sem)
    copy.start()
    copy.wait()


def cut(cells, start, size, after):
    anywhere = pl.BlockSpec(memory_space=pl.ANY)
    return pl.pallas_call(
        functools.partial(cut_kernel, start),
        grid=(1,),
        in_specs=[anywhere] * (1 + len(after)),
        out_specs=pl.BlockSpec((size, cells.shape[1]), lambda i: (0, 0)),
        out_shape=jax.ShapeDtypeStruct((size, cells.shape[1]), cells.dtype),
        scratch_shapes=[pltpu.SemaphoreType.DMA(())],
    )(cells, *after)


def gather_features(tokens, weight, sizes):
    found, start = [], 0
    for group in range(GROUPS[-1] + 1):
        members = [size for size, own in zip(sizes, GROUPS) if own == group]
        own = cut(tokens, start, sum(members), [weight] if start else [])
        full = lax.all_gather(own, "head", axis=1, tiled=True)
        found += [(full, sum(members[:i])) for i in range(len(members))]
        start += sum(members)
    return found


def per_device(tokens, proj_weight, partner_shard, partner_block):
    rows = tokens.shape[0]
    depth, heads, _ = proj_weight.shape
    blocks = rows // BLK
    count = lax.axis_size("ctx")
    me = lax.axis_index("ctx")
    span = rows * count
    weight_q = proj_weight[..., :HEAD_DIMENSION].reshape(depth, heads * HEAD_DIMENSION)
    weight_kv = proj_weight[..., HEAD_DIMENSION:].reshape(depth, heads * 2 * HEAD_DIMENSION)

    mine = me * blocks + jnp.arange(blocks)
    near = (mine[:, None] + jnp.array([-1, 0, 1])) % (count * blocks)
    fixed = jnp.concatenate(
        [near, jnp.broadcast_to(jnp.arange(GLOB)[None], (blocks, GLOB))], axis=1
    )
    partners = lax.dynamic_slice_in_dim(partner_shard * blocks + partner_block, me * blocks, blocks, 1)
    key_set = jnp.concatenate(
        [jnp.broadcast_to(fixed[None], (heads, blocks, 3 + GLOB)), partners], axis=2
    ).astype(jnp.int32)
    at = (((key_set // blocks) ^ me) * rows + (key_set % blocks) * BLK).astype(jnp.int32)

    parts, held, given, lead_queries = [], [], (), None
    queries, start = None, 0
    sizes = [rows * share // sum(PARTS) for share in PARTS]
    half = heads // 2 * HEAD_DIMENSION
    first = jnp.where(me == 1, heads // 2, 0).astype(jnp.int32).reshape(1)

    def placed(which):
        sources, places, start = [], [], 0
        for part in which:
            for run, at_row, cells in parts[part][0]:
                sources.append(cells)
                places.append(start + run * sizes[part] + at_row)
            start += sizes[part] * count
        return sources, places, start

    def at_home():
        sources, places, start = [], [], 0
        for size, part in zip(sizes, parts):
            for run, at_row, cells in part[0]:
                sources.append(cells)
                places.append(run * rows + start + at_row)
            start += size
        return sources, places, span

    at = at.reshape(-1)
    for part, (x, begin) in enumerate(gather_features(tokens, weight_kv, sizes)):
        fresh = part == 0 or GROUPS[part] > GROUPS[part - 1]
        near, far = parts[-1][1:] if parts else ([], [])
        settled = [cells for run, _, cells in parts[-2][0] if run] if part > 1 else []
        settled = settled + [lead_queries] * (part == 2)
        keyval = project(
            x,
            weight_kv,
            None,
            0,
            sizes[part],
            settled + (near if fresh else []) + ([] if queries is None or part == len(sizes) - 1 else [queries]),
        )
        ready, before = (far, []) if fresh else (near, far)
        keyval = after(keyval, *ready) if ready else keyval
        queries = project(x, weight_q, queries, start, rows, [keyval])
        if part == 0:
            got = lax.ppermute(queries[:LEAD, half:], "ctx", [(0, 1)])
            lead_queries = jnp.where(me == 1, got, queries[:LEAD, :half])
        if part == len(sizes) - 1:
            given = lead(first, lead_queries, *placed(range(part)), (), False)
            before = [given[0]] + before
        parts.append(spread(keyval, count, (), before))
        start += sizes[part]

    lead_own = lead(first, lead_queries, *placed([len(sizes) - 1]), given, True)
    lead_out = jnp.concatenate([lead_own, lax.ppermute(lead_own, "ctx", [(1, 0)])], axis=1)
    out = sparse(at, queries, *at_home(), [lead_own])
    out = out.reshape(rows, heads, HEAD_DIMENSION)
    lead_out = lead_out.reshape(LEAD, heads, HEAD_DIMENSION)
    return jnp.concatenate([jnp.where(me == 0, lead_out, out[:LEAD]), out[LEAD:]], axis=0)


def solution(mesh):
    in_specs = (
        P("ctx", "head"),
        P(None, "head", None),
        P("head", None, None),
        P("head", None, None),
    )
    out_specs = P("ctx", "head", None)
    return jax.shard_map(
        per_device, mesh=mesh, in_specs=in_specs, out_specs=out_specs, check_vma=False
    )
```
